512 devices in a mesh: bulk: 32 (over x, y), slide: 16 (over z, core).
Axes of the slice: x: 4, y: 8, z: 8, core: 2. Of those that a mesh axis runs over, the one named last changes fastest.
Arguments:
- tile_images: bfloat16 [16, 2048, 8, 8, 192], P('slide', 'bulk'), may hold values from -6 to 6
- destination: int32 [16, 2048], P('slide', 'bulk'), may hold values from -1 to 31, as said below
- encoder_slot: int32 [16, 2048], P('slide', 'bulk'), may hold values from -1 to 23, as said below
- tile_slide: int32 [16, 2048], P('slide', 'bulk'), may hold values from -1 to 3, as said below
- slide_tiles: int32 [16, 128], P('slide', 'bulk'), may hold values from 1 to 61, as said below
- targets: float32 [16, 128, 256], P('slide', 'bulk'), may hold values from -6 to 6
- depth_taps: float32 [49, 192], replicated, may hold values from -0.875 to 0.875
- first_proj: bfloat16 [192, 768], replicated, may hold values from -0.4375 to 0.4375
- second_proj: bfloat16 [768, 192], replicated, may hold values from -0.21875 to 0.21875
- reduce_proj: bfloat16 [768, 384], replicated, may hold values from -0.21875 to 0.21875
- head_proj: float32 [384, 256], replicated, may hold values from -0.3125 to 0.3125
Outputs:
- predictions: float32 [16, 128, 256], P('slide', 'bulk')
- embedding_cache: float32 [16, 768, 384], P('slide', 'bulk')
- grad_taps: float32 [49, 192], replicated
- grad_first: float32 [192, 768], replicated
- grad_second: float32 [768, 192], replicated
- grad_reduce: float32 [768, 384], replicated
The draws below stay inside these ranges and needn't reach their ends.
Inputs may be any that keep to these rules, and one draw needn't show every extreme that they name: `destination`: -1 marks an empty slot. In each replica every encoder index receives exactly 24 live tiles, at most 2 from the slots of one owner; in each replica some owner has all 64 slots live and sends exactly 2 to every encoder. `encoder_slot`: -1 exactly on empty slots; the 24 live tiles of one encoder in one replica carry the slot numbers 0 to 23 once each. `tile_slide`: -1 exactly on empty slots; every slide of every owner has one or more live tiles. `slide_tiles`: the number of live tiles of each slide; in each replica some slide has 61 of them.
All inputs are finite; a program needn't handle non-finite values.
Results may differ from the reference program's by a relative error of at most 0.006.
Values may be sent and summed in bfloat16 or wider, within the bound.
A program may use at most 128 MiB of HBM per device.

```python
import jax
import jax.numpy as jnp
from jax import lax

C1 = 192
HID = 768
C2 = 384
GENES = 256
KSIZE = 7
SIDE = 8
SLIDES_DEV = 4
TILE_CAP = 64
ENC_DEV = 24
SLIDES = 128
N_BULK = 32
N_SLIDE = 16


def replica_plan(key):
    key_loads, key_owner, key_encoder, key_extra, key_place = jax.random.split(key, 5)
    remaining = N_BULK * ENC_DEV - TILE_CAP
    baseline = remaining // (N_BULK - 1)
    spare = remaining % (N_BULK - 1)
    owners = jnp.arange(N_BULK, dtype=jnp.int32)
    loads = jnp.where(owners == 0, TILE_CAP, baseline + (owners - 1 < spare).astype(jnp.int32))
    reach = baseline - SLIDES_DEV
    shifts = jax.random.randint(key_loads, (N_BULK // 2 - 1,), -reach, reach + 1, dtype=jnp.int32)
    adjust = jnp.zeros((N_BULK,), jnp.int32).at[1:N_BULK - 1:2].add(shifts).at[2:N_BULK - 1:2].add(-shifts)
    loads = (loads + adjust)[jax.random.permutation(key_owner, N_BULK)]
    starts = jnp.cumsum(loads) - loads
    encoder_order = jax.random.permutation(key_encoder, N_BULK)
    within = jnp.arange(TILE_CAP, dtype=jnp.int32)
    global_pos = starts[:, None] + within[None, :]
    live = within[None, :] < loads[:, None]
    encoders = encoder_order[global_pos % N_BULK]
    enc_slots = global_pos // N_BULK
    extra = jax.random.randint(key_extra, (N_BULK, TILE_CAP), 0, SLIDES_DEV, dtype=jnp.int32)
    extra = jnp.where(loads[:, None] == TILE_CAP, 0, extra)
    slides = jnp.where(within[None, :] < SLIDES_DEV, within[None, :], extra)
    place = jax.vmap(lambda single: jax.random.permutation(single, TILE_CAP))(jax.random.split(key_place, N_BULK))
    live_slot = jnp.take_along_axis(live, place, axis=1)
    dest_out = jnp.where(live_slot, jnp.take_along_axis(encoders, place, axis=1), -1)
    slot_out = jnp.where(live_slot, jnp.take_along_axis(enc_slots, place, axis=1), -1)
    slide_out = jnp.where(live_slot, jnp.take_along_axis(slides, place, axis=1), -1)
    slide_range = jnp.arange(SLIDES_DEV, dtype=jnp.int32)
    counts = jnp.sum((slide_out[:, :, None] == slide_range[None, None, :]).astype(jnp.int32), axis=1)
    return (dest_out.reshape(-1).astype(jnp.int32), slot_out.reshape(-1).astype(jnp.int32), slide_out.reshape(-1).astype(jnp.int32), counts.reshape(-1).astype(jnp.int32))


def whole_plan(key):
    return jax.vmap(replica_plan)(jax.random.split(key, N_SLIDE))


def draw_destination(key, part):
    return whole_plan(key)[0]


def draw_encoder_slot(key, part):
    return whole_plan(key)[1]


def draw_tile_slide(key, part):
    return whole_plan(key)[2]


def draw_slide_tiles(key, part):
    return whole_plan(key)[3]


def block_levels(rng, extent, shards, smallest, largest):
    factor_of = 1.0
    for position, parts in shards:
        steps = jax.random.uniform(jax.random.fold_in(jax.random.fold_in(rng, 6), position), (parts,), jnp.float32, smallest / len(shards), largest / len(shards))
        factor_of = factor_of * jnp.repeat(jnp.exp(steps), extent[position] // parts).reshape((-1,) + (1,) * (len(extent) - 1 - position))
    return factor_of


def scatter_about(own_key, shape, spread, most, cuts=(), kind=jnp.bfloat16):
    array = spread * jax.random.normal(own_key, shape, jnp.float32)
    if cuts:
        array = array * block_levels(own_key, shape, cuts, -0.22, 0.18)
    return jnp.clip(array, -most, most).astype(kind)


def setup_inputs(seed: int = 0) -> dict:
    keys = jax.random.split(jax.random.key(seed), 12)
    return {
        "tile_images": scatter_about(keys[0], (N_SLIDE, N_BULK * TILE_CAP, SIDE, SIDE, C1), 1.0, 6.0, ((0, 16), (1, 32))),
        "destination": draw_destination(jax.random.fold_in(keys[11], 71), 0),
        "encoder_slot": draw_encoder_slot(jax.random.fold_in(keys[11], 71), 0),
        "tile_slide": draw_tile_slide(jax.random.fold_in(keys[11], 71), 0),
        "slide_tiles": draw_slide_tiles(jax.random.fold_in(keys[11], 71), 0),
        "targets": scatter_about(keys[5], (N_SLIDE, SLIDES, GENES), 1.0, 6.0, ((0, 16), (1, 32)), jnp.float32),
        "depth_taps": scatter_about(keys[6], (KSIZE * KSIZE, C1), (KSIZE * KSIZE) ** -0.5, 0.875, (), jnp.float32),
        "first_proj": scatter_about(keys[7], (C1, HID), C1 ** -0.5, 0.4375),
        "second_proj": scatter_about(keys[8], (HID, C1), HID ** -0.5, 0.21875),
        "reduce_proj": scatter_about(keys[9], (4 * C1, C2), (4 * C1) ** -0.5, 0.21875),
        "head_proj": scatter_about(keys[10], (C2, GENES), C2 ** -0.5, 0.3125, (), jnp.float32),
    }


norm_eps = 1e-06
root_half = 0.7071067811865476
normal_peak = 0.3989422804014327

def norm_rows(values):
    centered = values - lax.optimization_barrier(jnp.mean(values, axis=-1, keepdims=True))
    factor = lax.rsqrt(lax.optimization_barrier(jnp.mean(centered * centered, axis=-1, keepdims=True)) + norm_eps)
    return (centered * factor, factor)

def norm_back(normed, factor, incoming):
    return factor * (incoming - lax.optimization_barrier(jnp.mean(incoming, axis=-1, keepdims=True)) - normed * lax.optimization_barrier(jnp.mean(incoming * normed, axis=-1, keepdims=True)))

def gelu_exact(values):
    return 0.5 * values * (1.0 + lax.erf(values * root_half))

def gelu_slope(values):
    return 0.5 * (1.0 + lax.erf(values * root_half)) + values * jnp.exp(-0.5 * values * values) * normal_peak

def padded_float(images):
    margin = KSIZE // 2
    return jnp.pad(images.astype(jnp.float32), ((0, 0), (margin, margin), (margin, margin), (0, 0)))

def depthwise(padded, taps, side):
    total = jnp.zeros((padded.shape[0], side, side, padded.shape[3]), jnp.float32)
    for vertical in range(KSIZE):
        for lateral in range(KSIZE):
            total = total + padded[:, vertical:vertical + side, lateral:lateral + side, :] * taps[vertical * KSIZE + lateral]
    return total

def encode(images, taps, first_proj, second_proj, reduce_proj):
    count, side, _, chans = images.shape
    flat_rows = count * side * side
    inputs = images.astype(jnp.float32)
    spatial = depthwise(padded_float(images), taps, side)
    normed, first_factor = norm_rows(spatial)
    normed_low = normed.astype(jnp.bfloat16)
    hidden = jnp.dot(normed_low.reshape(flat_rows, chans), first_proj, preferred_element_type=jnp.float32)
    active = gelu_exact(hidden).astype(jnp.bfloat16)
    branch = jnp.dot(active, second_proj, preferred_element_type=jnp.float32)
    summed = inputs + branch.reshape(inputs.shape)
    second_normed, second_factor = norm_rows(summed)
    patches = lax.optimization_barrier(second_normed.astype(jnp.bfloat16)).astype(jnp.float32)
    blocks = patches.reshape(count, side // 2, 2, side // 2, 2, chans)
    pooled_patch = lax.optimization_barrier(jnp.mean(blocks, axis=(1, 3))).reshape(count, 4 * chans)
    reduced = jnp.dot(pooled_patch, reduce_proj.astype(jnp.float32), precision=lax.Precision.HIGHEST)
    embedded, third_factor = norm_rows(reduced)
    hidden_rows = hidden.reshape(count, side * side, hidden.shape[1])
    active_rows = active.reshape(count, side * side, active.shape[1])
    saved = (normed, first_factor, normed_low, hidden_rows, active_rows, second_normed, second_factor, pooled_patch, embedded, third_factor)
    return (embedded, saved)

def gradients(images, saved, cotangent, first_proj, second_proj, reduce_proj):
    normed, first_factor, normed_low, hidden_rows, active_rows, second_normed, second_factor, pooled_patch, embedded, third_factor = saved
    count, side, _, chans = images.shape
    flat_rows = count * side * side
    back_reduced = norm_back(embedded, third_factor, cotangent)
    grad_reduce = jnp.dot(pooled_patch.T, back_reduced, precision=lax.Precision.HIGHEST)
    back_patch = jnp.dot(back_reduced, reduce_proj.astype(jnp.float32).T, precision=lax.Precision.HIGHEST) / (side // 2 * (side // 2))
    back_blocks = jnp.broadcast_to(back_patch.reshape(count, 1, 2, 1, 2, chans), (count, side // 2, 2, side // 2, 2, chans)).reshape(count, side, side, chans)
    back_summed = norm_back(second_normed, second_factor, back_blocks)
    summed_low = back_summed.reshape(flat_rows, chans).astype(jnp.bfloat16)
    active = active_rows.reshape(flat_rows, active_rows.shape[2])
    hidden = hidden_rows.reshape(flat_rows, hidden_rows.shape[2])
    grad_second = jnp.dot(active.T, summed_low, preferred_element_type=jnp.float32)
    back_hidden = jnp.dot(summed_low, second_proj.T, preferred_element_type=jnp.float32) * gelu_slope(hidden)
    hidden_low = back_hidden.astype(jnp.bfloat16)
    grad_first = jnp.dot(normed_low.reshape(flat_rows, chans).T, hidden_low, preferred_element_type=jnp.float32)
    back_normed = jnp.dot(hidden_low, first_proj.T, preferred_element_type=jnp.float32).reshape(count, side, side, chans)
    back_spatial = norm_back(normed, first_factor, back_normed)
    padded = padded_float(images)
    tap_list = []
    for vertical in range(KSIZE):
        for lateral in range(KSIZE):
            window = padded[:, vertical:vertical + side, lateral:lateral + side, :]
            tap_list.append(lax.optimization_barrier(jnp.sum(window * back_spatial, axis=(0, 1, 2))))
    grad_taps = jnp.stack(tap_list, axis=0)
    return (grad_taps, grad_first, grad_second, grad_reduce)

def reference(tile_images, destination, encoder_slot, tile_slide, slide_tiles, targets, depth_taps, first_proj, second_proj, reduce_proj, head_proj):
    live_total = N_BULK * ENC_DEV

    def replica(carry, inputs):
        images, dest_rows, slot_rows, slide_rows, count_rows, target_rows = inputs
        total_slots = images.shape[0]
        order_key = jnp.where(dest_rows >= 0, dest_rows * ENC_DEV + slot_rows, live_total + jnp.arange(total_slots).astype(jnp.int32)).astype(jnp.int32)
        order = jnp.argsort(order_key, stable=True)[:live_total].astype(jnp.int32)
        working = images[order]
        slide_global = (order // TILE_CAP * SLIDES_DEV + slide_rows[order]).astype(jnp.int32)
        embedded, saved = encode(working, depth_taps, first_proj, second_proj, reduce_proj)
        slide_range = jnp.arange(N_BULK * SLIDES_DEV).astype(jnp.int32)
        member = (slide_global[None, :] == slide_range[:, None]).astype(jnp.float32)
        counts = count_rows.astype(jnp.float32)[:, None]
        pooled = jnp.dot(member, embedded, precision=lax.Precision.HIGHEST) / counts
        predicted = jnp.dot(pooled, head_proj, precision=lax.Precision.HIGHEST)
        back_pooled = jnp.dot(predicted - target_rows, head_proj.T, precision=lax.Precision.HIGHEST) / counts
        back_rows = jnp.dot(member.T, back_pooled, precision=lax.Precision.HIGHEST)
        found = gradients(working, saved, back_rows, first_proj, second_proj, reduce_proj)
        updated = tuple((first + second for first, second in zip(carry, found)))
        return (updated, (predicted, embedded))
    start = (jnp.zeros(depth_taps.shape, jnp.float32), jnp.zeros(first_proj.shape, jnp.float32), jnp.zeros(second_proj.shape, jnp.float32), jnp.zeros(reduce_proj.shape, jnp.float32))
    totals, stacked = lax.scan(replica, start, (tile_images, destination, encoder_slot, tile_slide, slide_tiles, targets))
    return (stacked[0], stacked[1], totals[0], totals[1], totals[2], totals[3])
```

```python
import functools
import jax
import jax.numpy as jnp
from jax import lax
from jax.experimental import pallas as pl
from jax.experimental.pallas import tpu as pltpu
from jax.sharding import PartitionSpec as P

F32 = jnp.float32
BF = jnp.bfloat16
TILES = 64
CHANS = 192
HIDDEN = 768
WIDTH = 384
GROUPS = 6
PLANE = 8 * TILES
norm_eps = 1e-06


def dot(a, b):
    return jnp.dot(a, b, preferred_element_type=F32)


def dot_nt(a, b):
    return lax.dot_general(a, b, (((1,), (1,)), ((), ())), preferred_element_type=F32)


def dot_tn(a, b):
    return lax.dot_general(a, b, (((0,), (0,)), ((), ())), preferred_element_type=F32)


def parts_of(values):
    high = values.astype(BF)
    rest = values - high.astype(F32)
    middle = rest.astype(BF)
    low = (rest - middle.astype(F32)).astype(BF)
    return high, middle, low


def lane_mean(values):
    return jnp.sum(values, axis=-1, keepdims=True) * (1.0 / values.shape[-1])


def norm_rows(values):
    centered = values - lane_mean(values)
    factor = lax.rsqrt(lane_mean(centered * centered) + norm_eps)
    return centered * factor, factor


def gelu_pair(h):
    size = jnp.abs(h)
    bell = jnp.exp(h * h * -0.5)
    t = 1.0 / (1.0 + (0.3275911 * 0.7071067811865476) * size)
    poly = t * (
        0.5 * 0.254829592
        + t
        * (
            0.5 * -0.284496736
            + t * (0.5 * 1.421413741 + t * (0.5 * -1.453152027 + t * (0.5 * 1.061405429)))
        )
    )
    tail = poly * bell
    phi = jnp.where(h >= 0, 1.0 - tail, tail)
    return h * phi, phi + h * bell * 0.3989422804014327


def gelu_pair_erf(h):
    phi = 0.5 * (1.0 + lax.erf(h * 0.7071067811865476))
    return h * phi, phi + h * jnp.exp(h * h * -0.5) * 0.3989422804014327


GELU = gelu_pair


def blocks_of_lanes(rows):
    return lax.broadcasted_iota(jnp.int32, (rows, 128), 1) // 32


def to_groups(source, target, row0):
    block = blocks_of_lanes(TILES)

    def step(i, carry):
        for t in range(2):
            tiles = []
            for jm in range(4):
                rows = pl.ds((4 * t + jm) * PLANE + i * TILES, TILES)
                tiles.append((source[rows, 0:128], source[rows, 128:256]))
            for g in range(GROUPS):
                total = None
                for jm in range(4):
                    shift = 32 * ((jm - g % 4) % 4)
                    piece = tiles[jm][g // 4]
                    if shift:
                        piece = pltpu.roll(piece, shift, 1)
                    total = piece if total is None else jnp.where(block == jm, piece, total)
                target[g, pl.ds(row0 + i * TILES, TILES), t * 128 : (t + 1) * 128] = total.astype(BF)
        return carry

    lax.fori_loop(0, 8, step, 0)


def compute_kernel(
    x_ref, taps_ref, w1_ref, w2t_ref, wr_ref, head_ref, dest_ref, slot_ref, slide_ref, count_ref, targets_ref,
    pred_ref, send_ref, pack_ref,
    g1_ref, g2_ref, gr_ref, low_ref, high_ref, xs_ref, xg_ref, xt_ref, wd_ref, tg_ref, y_ref, n_ref, nb_ref,
    gb_ref, sl_ref, m_ref, pm_ref, w1t_ref, w2_ref, bp_ref, fold_ref,
):
    f1_ref, f2_ref, gy_ref = low_ref, high_ref, xs_ref

    def widen(k, carry):
        rows = pl.ds(k * 512, 512)
        values = x_ref[rows, :].astype(F32)
        low_ref[rows, :] = values[:, 0:128]
        high_ref[rows, 0:64] = values[:, 128:192]
        return carry

    lax.fori_loop(0, 8, widen, 0)

    def regroup(i, carry):
        for j in range(8):
            rows = pl.ds(j * PLANE + i * TILES, TILES)
            xs_ref[rows, 0:128] = low_ref[pl.ds(i * 8 + j, TILES, stride=64), :]
            xs_ref[rows, 128:256] = high_ref[pl.ds(i * 8 + j, TILES, stride=64), :]
        return carry

    lax.fori_loop(0, 8, regroup, 0)

    xg_ref[:, 0 : 3 * TILES, :] = jnp.zeros((GROUPS, 3 * TILES, 256), BF)
    xg_ref[:, 11 * TILES : 14 * TILES, :] = jnp.zeros((GROUPS, 3 * TILES, 256), BF)
    to_groups(xs_ref, xg_ref, 3 * TILES)

    block56 = blocks_of_lanes(56)
    taps_low = taps_ref[:, 0:128]
    taps_high = taps_ref[:, 128:256]
    for g in range(GROUPS):
        source = taps_low if g < 4 else taps_high
        total = None
        for jm in range(4):
            shift = 32 * ((jm - g % 4) % 4)
            piece = pltpu.roll(source, shift, 1) if shift else source
            total = piece if total is None else jnp.where(block56 == jm, piece, total)
        for a in range(7):
            tg_ref[g, a, 0:4, :] = jnp.zeros((4, 128), F32)
            tg_ref[g, a, 4:11, :] = total[a * 7 : a * 7 + 7, :]
            tg_ref[g, a, 11:16, :] = jnp.zeros((5, 128), F32)
    same = lax.broadcasted_iota(jnp.int32, (32, 128), 0) == lax.broadcasted_iota(jnp.int32, (32, 128), 1) % 32
    block32 = blocks_of_lanes(32)

    def bands(g):
        for a in range(7):
            for d in range(-4, 8):
                total = None
                for jm in range(4):
                    b = d - jm + 3
                    if b < 0 or b > 6:
                        continue
                    row = jnp.broadcast_to(tg_ref[g, a, 4 + b : 5 + b, :], (32, 128))
                    keep = same & (block32 == jm)
                    total = jnp.where(keep, row, 0.0) if total is None else jnp.where(keep, row, total)
                if total is None:
                    total = jnp.zeros((32, 128), F32)
                pieces = parts_of(total)[:SPLIT]
                for p in range(SPLIT):
                    if d >= 0:
                        wd_ref[a, p, d * 32 : d * 32 + 32, 0:128] = pieces[p]
                    if d + 4 < 8:
                        wd_ref[a, p, (d + 4) * 32 : (d + 4) * 32 + 32, 128:256] = pieces[p]

    def convolve(g, carry):
        bands(g)
        total = None
        for a in range(7):
            lhs = xg_ref[g, a * TILES : a * TILES + PLANE, :]
            for p in range(SPLIT):
                found = dot(lhs, wd_ref[a, p])
                total = found if total is None else total + found
        y_ref[g] = total
        xt_ref[g, 0, :, 128:768] = jnp.transpose(xg_ref[g, 128:768, :], (1, 0))
        xt_ref[g, 1, :, 128:640] = jnp.transpose(xg_ref[g, 192:704, :], (1, 0))
        xt_ref[g, 0, :, 0:128] = jnp.zeros((256, 128), BF)
        xt_ref[g, 0, :, 768:896] = jnp.zeros((256, 128), BF)
        xt_ref[g, 1, :, 0:128] = jnp.zeros((256, 128), BF)
        xt_ref[g, 1, :, 640:896] = jnp.zeros((256, 256), BF)
        return carry

    lax.fori_loop(0, GROUPS, convolve, 0)

    block64 = blocks_of_lanes(TILES)

    def first_norm(i, carry):
        rows = pl.ds(i * TILES, TILES)
        for t in range(2):
            tiles = [y_ref[g, rows, t * 128 : (t + 1) * 128] for g in range(GROUPS)]
            for jm in range(4):
                halves = []
                for picks in ((0, 1, 2, 3), (4, 5)):
                    total = None
                    for g in picks:
                        shift = 32 * ((g % 4 - jm) % 4)
                        piece = pltpu.roll(tiles[g], shift, 1) if shift else tiles[g]
                        total = piece if total is None else jnp.where(block64 == g % 4, piece, total)
                    halves.append(total)
                halves[1] = jnp.where(block64 < 2, halves[1], 0.0)
                mean = jnp.sum(halves[0] + halves[1], axis=-1, keepdims=True) * (1.0 / CHANS)
                c0 = halves[0] - mean
                c1 = jnp.where(block64 < 2, halves[1] - mean, 0.0)
                factor = lax.rsqrt(jnp.sum(c0 * c0 + c1 * c1, axis=-1, keepdims=True) * (1.0 / CHANS) + norm_eps)
                where = pl.ds((4 * t + jm) * PLANE + i * TILES, TILES)
                n0 = c0 * factor
                n1 = c1 * factor
                n_ref[where, 0:128] = n0
                n_ref[where, 128:256] = n1
                nb_ref[where, 0:128] = n0.astype(BF)
                nb_ref[where, 128:256] = n1.astype(BF)
                f1_ref[where, :] = jnp.broadcast_to(factor, (TILES, 128))
        return carry

    lax.fori_loop(0, 8, first_norm, 0)

    pm_ref[...] = jnp.zeros_like(pm_ref)
    w1t_ref[...] = jnp.transpose(w1_ref[...], (1, 0))
    w2_ref[...] = jnp.transpose(w2t_ref[...], (1, 0))

    def block_step(k, carry):
        rows = pl.ds(k * CH, CH)
        low = nb_ref[rows, 0:CHANS]
        branch = None
        for part in range(HIDDEN // HP):
            cols = slice(part * HP, part * HP + HP)
            hidden = dot(low, w1_ref[:, cols])
            active, slope = GELU(hidden)
            active = active.astype(BF)
            gb_ref[rows, cols] = active
            sl_ref[rows, cols] = slope.astype(BF)
            found = dot(active, w2_ref[cols, :])
            branch = found if branch is None else branch + found
        summed = xs_ref[rows, 0:CHANS] + branch
        normed, factor = norm_rows(summed)
        m_ref[rows, 0:CHANS] = normed
        f2_ref[rows, :] = jnp.broadcast_to(factor, (CH, 128))
        rounded = normed.astype(BF).astype(F32)
        lateral = lax.rem(k // (PLANE // CH), 2)
        for u in range(2):
            total = None
            for i in range(u, CH // TILES, 2):
                piece = rounded[i * TILES : (i + 1) * TILES, :]
                total = piece if total is None else total + piece
            pm_ref[u, lateral] += total
        return carry

    lax.fori_loop(0, 8 * PLANE // CH, block_step, 0)

    pooled = [pm_ref[u, v] * (1.0 / 16.0) for u in range(2) for v in range(2)]
    split = [parts_of(piece) for piece in pooled]
    reduced = None
    for q in range(4):
        stacked = jnp.concatenate(split[q], axis=0)
        found = dot(stacked, wr_ref[q * CHANS : (q + 1) * CHANS, :])
        found = found[0:TILES] + found[TILES : 2 * TILES] + found[2 * TILES :]
        reduced = found if reduced is None else reduced + found
    embedded, third = norm_rows(reduced)
    slide_row = slide_ref[...]
    member = (slide_row == lax.broadcasted_iota(jnp.int32, (8, TILES), 0)).astype(F32)
    eye = lax.broadcasted_iota(jnp.int32, (TILES, TILES), 0) == lax.broadcasted_iota(jnp.int32, (TILES, TILES), 1)
    eye8 = lax.broadcasted_iota(jnp.int32, (8, 8), 0) == lax.broadcasted_iota(jnp.int32, (8, 8), 1)
    counts = jnp.sum(jnp.where(eye8, jnp.broadcast_to(count_ref[...].astype(F32), (8, 8)), 0.0), axis=1, keepdims=True)
    exact = functools.partial(jnp.dot, precision=lax.Precision.HIGHEST, preferred_element_type=F32)
    pooled_slides = exact(member, embedded) / counts
    predicted = exact(pooled_slides, head_ref[...])
    pred_ref[...] = predicted[0:4]
    missed = predicted[0:4] - targets_ref[...]
    missed = jnp.concatenate([missed, jnp.zeros((4, missed.shape[1]), F32)], axis=0)
    back_pooled = (
        lax.dot_general(
            missed, head_ref[...], (((1,), (1,)), ((), ())), precision=lax.Precision.HIGHEST, preferred_element_type=F32
        )
        / counts
    )
    cotangent = lax.dot_general(
        member, back_pooled, (((0,), (0,)), ((), ())), precision=lax.Precision.HIGHEST, preferred_element_type=F32
    )
    back = third * (cotangent - lane_mean(cotangent) - embedded * lane_mean(cotangent * embedded))
    back_parts = parts_of(back)
    stacked_back = jnp.concatenate(back_parts, axis=0)
    for q in range(4):
        piece = dot_nt(stacked_back, wr_ref[q * CHANS : (q + 1) * CHANS, :])
        piece = (piece[0:TILES] + piece[TILES : 2 * TILES] + piece[2 * TILES :]) * (1.0 / 16.0)
        bp_ref[q // 2, q % 2] = piece
        rows_q = jnp.concatenate([split[q][0], split[q][1], split[q][0]], axis=0)
        cols_q = jnp.concatenate([back_parts[0], back_parts[0], back_parts[1]], axis=0)
        gr_ref[q * CHANS : (q + 1) * CHANS, :] = dot_tn(rows_q, cols_q)

    dest_row = dest_ref[...]
    dest_col = jnp.sum(jnp.where(eye, jnp.broadcast_to(dest_row, (TILES, TILES)).astype(F32), 0.0), axis=1, keepdims=True)
    first_index = lax.broadcasted_iota(jnp.int32, (TILES, TILES), 0)
    second_index = lax.broadcasted_iota(jnp.int32, (TILES, TILES), 1)
    dest_f = dest_row.astype(F32)
    earlier = (dest_col == dest_f) & (first_index < second_index)
    rank = jnp.sum(earlier.astype(F32), axis=0, keepdims=True)
    slot_f = slot_ref[...].astype(F32) + 1.0
    slot_col = jnp.sum(jnp.where(eye, jnp.broadcast_to(slot_f, (TILES, TILES)), 0.0), axis=1, keepdims=True)
    emb_parts = parts_of(embedded)
    peer = lax.broadcasted_iota(jnp.int32, (32, TILES), 0).astype(F32)
    for r in range(2):
        choose = ((peer == dest_f) & (rank == float(r))).astype(BF)
        picked = dot(choose, emb_parts[0]) + dot(choose, emb_parts[1]) + dot(choose, emb_parts[2])
        for q in range(3):
            send_ref[pl.ds(r * 4 + q, 32, stride=8), :] = picked[:, q * 128 : (q + 1) * 128]
        send_ref[pl.ds(r * 4 + 3, 32, stride=8), :] = dot(choose, jnp.broadcast_to(slot_col, (TILES, 128)).astype(BF))

    g1_ref[...] = jnp.zeros_like(g1_ref)
    g2_ref[...] = jnp.zeros_like(g2_ref)

    def back_step(k, carry):
        rows = pl.ds(k * CH, CH)
        lateral = lax.rem(k // (PLANE // CH), 2)
        patch = [bp_ref[u, lateral] for u in range(2)]
        incoming = jnp.concatenate([patch[i % 2] for i in range(CH // TILES)], axis=0)
        normed = m_ref[rows, 0:CHANS]
        factor = f2_ref[rows, 0:1]
        back_sum = factor * (incoming - lane_mean(incoming) - normed * lane_mean(incoming * normed))
        low = back_sum.astype(BF)
        active = gb_ref[rows, :]
        g2_ref[...] += dot_tn(low, active)
        nb = nb_ref[rows, 0:CHANS]
        normal = None
        for part in range(HIDDEN // HP):
            cols = slice(part * HP, part * HP + HP)
            back_hidden = (dot(low, w2t_ref[:, cols]) * sl_ref[rows, cols].astype(F32)).astype(BF)
            g1_ref[:, cols] += dot_tn(nb, back_hidden)
            found = dot(back_hidden, w1t_ref[cols, :])
            normal = found if normal is None else normal + found
        n = n_ref[rows, 0:CHANS]
        f1 = f1_ref[rows, 0:1]
        gy_ref[rows, 0:CHANS] = f1 * (normal - lane_mean(normal) - n * lane_mean(normal * n))
        return carry

    lax.fori_loop(0, 8 * PLANE // CH, back_step, 0)

    to_groups(gy_ref, xg_ref, 0)
    block8 = blocks_of_lanes(8)
    same8 = [
        (lax.broadcasted_iota(jnp.int32, (8, 128), 0) + 8 * v) == lax.broadcasted_iota(jnp.int32, (8, 128), 1) % 32
        for v in range(4)
    ]

    def tap_step(g, carry):
        right = xg_ref[g, 0:PLANE, :]
        for a in range(7):
            lane0 = (a * TILES) // 128 * 128
            left = xt_ref[g, a % 2, :, lane0 : lane0 + PLANE]
            found = dot(left, right)
            sums = {}
            for j in range(8):
                for t in range(2):
                    total = None
                    for v in range(4):
                        piece = found[j * 32 + v * 8 : j * 32 + v * 8 + 8, t * 128 : (t + 1) * 128]
                        piece = jnp.where(same8[v], piece, 0.0)
                        total = piece if total is None else total + piece
                    sums[j, t] = total
            for b in range(7):
                total = None
                for t in range(2):
                    inner = jnp.zeros((8, 128), F32)
                    for jm in range(4):
                        j = 4 * t + jm + b - 3
                        if 0 <= j < 8:
                            inner = jnp.where(block8 == jm, sums[j, t], inner)
                    total = inner if total is None else total + inner
                total = total + pltpu.roll(total, 64, 1)
                total = total + pltpu.roll(total, 32, 1)
                fold_ref[g, a * 7 + b : a * 7 + b + 1, :] = jnp.sum(total, axis=0, keepdims=True)
        return carry

    lax.fori_loop(0, GROUPS, tap_step, 0)
    block49 = blocks_of_lanes(56)
    for half, picks in enumerate(((0, 1, 2, 3), (4, 5))):
        total = jnp.zeros((56, 128), F32)
        for g in picks:
            total = jnp.where(block49 == g % 4, fold_ref[g], total)
        for band in range(7):
            pack_ref[band * 2 + half, 72:80, :] = total[band * 8 : band * 8 + 8, :]
    pack_ref[14:64, 72:80, :] = jnp.zeros((50, 8, 128), F32)
    for k in range(32):
        for l in range(3):
            pack_ref[k, l * 24 : l * 24 + 24, :] = gr_ref[k * 24 : k * 24 + 24, l * 128 : l * 128 + 128]
    for k in range(16):
        for l in range(3):
            lane = (k % 2) * 384 + l * 128
            row = k // 2 * 24
            pack_ref[32 + k, l * 24 : l * 24 + 24, :] = g1_ref[row : row + 24, lane : lane + 128]
            pack_ref[48 + k, l * 24 : l * 24 + 24, :] = g2_ref[row : row + 24, lane : lane + 128]


SPLIT = 2
CH = 512
HP = 256


def compute(x, taps, w1, w2t, wr, head, dest, slot, slide, count, targets):
    shapes = (
        jax.ShapeDtypeStruct((4, 256), F32),
        jax.ShapeDtypeStruct((256, 128), F32),
        jax.ShapeDtypeStruct((64, 80, 128), F32),
    )
    rows = 8 * PLANE
    scratch = [
        pltpu.VMEM((CHANS, HIDDEN), F32),
        pltpu.VMEM((CHANS, HIDDEN), F32),
        pltpu.VMEM((4 * CHANS, WIDTH), F32),
        pltpu.VMEM((rows, 128), F32),
        pltpu.VMEM((rows, 128), F32),
        pltpu.VMEM((rows, 256), F32),
        pltpu.VMEM((GROUPS, 14 * TILES, 256), BF),
        pltpu.VMEM((GROUPS, 2, 256, 896), BF),
        pltpu.VMEM((7, SPLIT, 256, 256), BF),
        pltpu.VMEM((GROUPS, 7, 16, 128), F32),
        pltpu.VMEM((GROUPS, PLANE, 256), F32),
        pltpu.VMEM((rows, 256), F32),
        pltpu.VMEM((rows, 256), BF),
        pltpu.VMEM((rows, HIDDEN), BF),
        pltpu.VMEM((rows, HIDDEN), BF),
        pltpu.VMEM((rows, 256), F32),
        pltpu.VMEM((2, 2, TILES, CHANS), F32),
        pltpu.VMEM((HIDDEN, CHANS), BF),
        pltpu.VMEM((HIDDEN, CHANS), BF),
        pltpu.VMEM((2, 2, TILES, CHANS), F32),
        pltpu.VMEM((GROUPS, 56, 128), F32),
    ]
    return pl.pallas_call(
        compute_kernel,
        out_shape=shapes,
        in_specs=[pl.BlockSpec(memory_space=pltpu.VMEM)] * 11,
        out_specs=tuple(pl.BlockSpec(memory_space=pltpu.VMEM) for _ in shapes),
        scratch_shapes=scratch,
        compiler_params=pltpu.CompilerParams(vmem_limit_bytes=62 * 1024 * 1024),
        name="encode_and_gradients",
    )(x, taps, w1, w2t, wr, head, dest, slot, slide, count, targets)


def sum_kernel(pack_ref, send_ref, all_ref, got_ref, core_out, core_in, own_ref, x_out, x_in, y_out, y_in, z_out, z_in, send_sems, recv_sems):
    bulk = lax.axis_index("bulk")
    slide = lax.axis_index("slide")
    x, y = bulk // 8, bulk % 8
    z, core = slide // 2, slide % 2

    def place(bx, by, bz, bc):
        return (bx * 8 + by, bz * 2 + bc)

    mate = place(x, y, z, 1 - core)
    x_peers = [((x + o) % 4) for o in range(1, 4)]
    y_peers = [((y + o) % 8) for o in range(1, 8)]
    z_peers = [((z + o) % 8) for o in range(1, 8)]
    b_peers = [((bulk + o) % 32) for o in range(1, 32)]
    barrier = pltpu.get_barrier_semaphore()
    everyone = [mate] + [(b, slide) for b in b_peers] + [place(x, y, p, core) for p in z_peers]
    for device in everyone:
        pl.semaphore_signal(barrier, inc=1, device_id=device, device_id_type=pl.DeviceIdType.MESH)
    counter = [0]

    def copy(source, target, device):
        k = counter[0]
        counter[0] += 1
        made = pltpu.make_async_remote_copy(
            src_ref=source, dst_ref=target, send_sem=send_sems.at[k], recv_sem=recv_sems.at[k],
            device_id=device, device_id_type=pl.DeviceIdType.MESH,
        )
        made.start()
        return made

    def finish(copies):
        for made in copies:
            made.wait_recv()

    def pack(k, carry):
        core_out[k] = pack_ref[(1 - core) * 32 + k].astype(BF)
        return carry

    lax.fori_loop(0, 32, pack, 0, unroll=8)
    pl.semaphore_wait(barrier, len(everyone))
    started = [copy(core_out, core_in, mate)]
    tiles = [copy(send_ref.at[p], got_ref.at[bulk], (p, slide)) for p in b_peers]
    got_ref[bulk] = send_ref[bulk]
    finish(started)

    def add_core(k, carry):
        total = pack_ref[core * 32 + k] + core_in[k].astype(F32)
        own_ref[k] = total
        x_out[k // 8, k % 8] = total.astype(BF)
        return carry

    lax.fori_loop(0, 32, add_core, 0, unroll=8)
    step = [copy(x_out.at[p], x_in.at[o], place(p, y, z, core)) for o, p in enumerate(x_peers)]
    started += step
    finish(step)

    def add_x(k, carry):
        total = own_ref[x * 8 + k]
        for o in range(3):
            total = total + x_in[o, k].astype(F32)
        y_out[k] = total.astype(YT)
        return carry

    lax.fori_loop(0, 8, add_x, 0, unroll=4)
    step = [copy(y_out.at[p], y_in.at[o], place(x, p, z, core)) for o, p in enumerate(y_peers)]
    started += step
    finish(step)
    total = y_out[y].astype(F32)
    for o in range(7):
        total = total + y_in[o].astype(F32)
    z_out[...] = total.astype(ZT)
    step = [copy(z_out, z_in.at[z], place(x, y, p, core)) for p in z_peers]
    started += step
    z_in[z] = z_out[...]
    finish(step)
    total = z_in[0].astype(F32)
    for o in range(1, 8):
        total = total + z_in[o].astype(F32)
    mine = core * 32 + x * 8 + y
    all_ref[mine] = total.astype(BF)
    step = [copy(all_ref.at[mine], all_ref.at[mine], place(x, p, z, core)) for p in y_peers]
    started += step
    finish(step)
    row = all_ref.at[pl.ds(core * 32 + x * 8, 8)]
    step = [copy(row, row, place(p, y, z, core)) for p in x_peers]
    started += step
    finish(step)
    half = all_ref.at[pl.ds(core * 32, 32)]
    step = [copy(half, half, mate)]
    started += step
    finish(step)
    finish(tiles)
    for made in started + tiles:
        made.wait_send()


YT = F32
ZT = F32


def sum_everywhere(pack, send):
    vmem = pl.BlockSpec(memory_space=pltpu.VMEM)
    return pl.pallas_call(
        sum_kernel,
        out_shape=(jax.ShapeDtypeStruct((64, 80, 128), BF), jax.ShapeDtypeStruct((32, 8, 128), F32)),
        in_specs=[vmem, vmem],
        out_specs=(vmem, vmem),
        scratch_shapes=[
            pltpu.VMEM((32, 80, 128), BF),
            pltpu.VMEM((32, 80, 128), BF),
            pltpu.VMEM((32, 80, 128), F32),
            pltpu.VMEM((4, 8, 80, 128), BF),
            pltpu.VMEM((3, 8, 80, 128), BF),
            pltpu.VMEM((8, 80, 128), YT),
            pltpu.VMEM((7, 80, 128), YT),
            pltpu.VMEM((80, 128), ZT),
            pltpu.VMEM((8, 80, 128), ZT),
            pltpu.SemaphoreType.DMA((60,)),
            pltpu.SemaphoreType.DMA((60,)),
        ],
        compiler_params=pltpu.CompilerParams(
            collective_id=0, has_side_effects=True, vmem_limit_bytes=40 * 1024 * 1024
        ),
        name="sum_gradients",
    )(pack, send.reshape(32, 8, 128))


def unpack_kernel(all_ref, got_ref, cache_ref, gt_ref, g1_ref, g2_ref, gr_ref):
    for k in range(32):
        values = all_ref[k, 0:72, :].astype(F32)
        for l in range(3):
            gr_ref[k * 24 : k * 24 + 24, l * 128 : l * 128 + 128] = values[l * 24 : l * 24 + 24]
    for k in range(16):
        first = all_ref[32 + k, 0:72, :].astype(F32)
        second = all_ref[48 + k, 0:72, :].astype(F32)
        for l in range(3):
            lane = (k % 2) * 384 + l * 128
            row = k // 2 * 24
            g1_ref[row : row + 24, lane : lane + 128] = first[l * 24 : l * 24 + 24]
            g2_ref[row : row + 24, lane : lane + 128] = second[l * 24 : l * 24 + 24]
    for band in range(7):
        left = all_ref[band * 2].astype(F32)[72:80]
        right = all_ref[band * 2 + 1].astype(F32)[72:80]
        count = 8 if band < 6 else 1
        gt_ref[band * 8 : band * 8 + count, 0:128] = left[0:count]
        gt_ref[band * 8 : band * 8 + count, 128:192] = right[0:count, 0:64]
    cache = [jnp.zeros((24, 128), F32) for _ in range(3)]
    for r in range(2):
        slots = jnp.transpose(got_ref[pl.ds(r * 4 + 3, 32, stride=8), :], (1, 0))[0:24]
        wanted = (lax.broadcasted_iota(jnp.int32, (24, 32), 0) + 1).astype(F32)
        choose = (slots == wanted).astype(BF)
        for q in range(3):
            for piece in parts_of(got_ref[pl.ds(r * 4 + q, 32, stride=8), :]):
                cache[q] = cache[q] + dot(choose, piece)
    for q in range(3):
        cache_ref[:, q * 128 : (q + 1) * 128] = cache[q]


def unpack(everything, got):
    vmem = pl.BlockSpec(memory_space=pltpu.VMEM)
    return pl.pallas_call(
        unpack_kernel,
        out_shape=(
            jax.ShapeDtypeStruct((24, WIDTH), F32),
            jax.ShapeDtypeStruct((49, CHANS), F32),
            jax.ShapeDtypeStruct((CHANS, HIDDEN), F32),
            jax.ShapeDtypeStruct((CHANS, HIDDEN), F32),
            jax.ShapeDtypeStruct((4 * CHANS, WIDTH), F32),
        ),
        in_specs=[vmem, vmem],
        out_specs=(vmem,) * 5,
        compiler_params=pltpu.CompilerParams(vmem_limit_bytes=40 * 1024 * 1024),
        name="unpack_gradients",
    )(everything, got.reshape(256, 128))


def prepare(tile_images, destination, encoder_slot, tile_slide, slide_tiles, targets, depth_taps, first_proj, second_proj, reduce_proj, head_proj):
    x = tile_images.reshape(TILES * 64, CHANS)
    taps = jnp.pad(depth_taps, ((0, 7), (0, 64)))
    count = jnp.pad(slide_tiles.reshape(1, 4), ((0, 0), (0, 4)), constant_values=1)
    return (x, taps, first_proj, second_proj.T, reduce_proj, head_proj, destination.reshape(1, TILES),
            encoder_slot.reshape(1, TILES), tile_slide.reshape(1, TILES), count, targets.reshape(4, 256))


def local(*arguments):
    predicted, send, pack = compute(*prepare(*arguments))
    everything, got = sum_everywhere(pack, send)
    cache, gt, g1, g2, gr = unpack(everything, got)
    return predicted[None], cache[None], gt, g1, g2.T, gr


def solution(mesh):
    in_specs = (
        P("slide", "bulk", None, None, None),
        P("slide", "bulk"),
        P("slide", "bulk"),
        P("slide", "bulk"),
        P("slide", "bulk"),
        P("slide", "bulk", None),
        P(),
        P(),
        P(),
        P(),
        P(),
    )
    out_specs = (P("slide", "bulk", None), P("slide", "bulk", None), P(), P(), P(), P())
    return jax.shard_map(local, mesh=mesh, in_specs=in_specs, out_specs=out_specs, check_vma=False)
```

```python
import functools
import jax
import jax.numpy as jnp
from jax import lax
from jax.experimental import pallas as pl
from jax.experimental.pallas import tpu as pltpu
from jax.sharding import PartitionSpec as P

F32 = jnp.float32
BF = jnp.bfloat16
TILES = 64
CHANS = 192
HIDDEN = 768
WIDTH = 384
GROUPS = 6
PLANE = 8 * TILES
norm_eps = 1e-06


def dot(a, b):
    return jnp.dot(a, b, preferred_element_type=F32)


def dot_nt(a, b):
    return lax.dot_general(a, b, (((1,), (1,)), ((), ())), preferred_element_type=F32)


def dot_tn(a, b):
    return lax.dot_general(a, b, (((0,), (0,)), ((), ())), preferred_element_type=F32)


def parts_of(values):
    high = values.astype(BF)
    rest = values - high.astype(F32)
    middle = rest.astype(BF)
    low = (rest - middle.astype(F32)).astype(BF)
    return high, middle, low


def lane_mean(values):
    return jnp.sum(values, axis=-1, keepdims=True) * (1.0 / values.shape[-1])


def norm_rows(values):
    centered = values - lane_mean(values)
    factor = lax.rsqrt(lane_mean(centered * centered) + norm_eps)
    return centered * factor, factor


def gelu_pair(h):
    phi = 0.5 * (1.0 + lax.erf(h * 0.7071067811865476))
    return h * phi, phi + h * jnp.exp(h * h * -0.5) * 0.3989422804014327


SKIP = ()


def loop(count, body):
    if body.__name__ not in SKIP:
        lax.fori_loop(0, count, body, 0)


def same_block(extent, size):
    first = lax.broadcasted_iota(jnp.int32, (extent, extent), 0) // size
    return first == lax.broadcasted_iota(jnp.int32, (extent, extent), 1) // size


def sum_by(values, ones, passes):
    high = values.astype(BF)
    total = dot(high, ones)
    if passes > 1:
        total = total + dot((values - high.astype(F32)).astype(BF), ones)
    return total


def blocks_of_lanes(rows):
    return lax.broadcasted_iota(jnp.int32, (rows, 128), 1) // 32


def to_groups(source, target, row0):
    block = blocks_of_lanes(TILES)

    def step(i, carry):
        for t in range(2):
            tiles = []
            for jm in range(4):
                rows = pl.ds((4 * t + jm) * PLANE + i * TILES, TILES)
                tiles.append((source[rows, 0:128], source[rows, 128:256]))
            for g in range(GROUPS):
                total = None
                for jm in range(4):
                    shift = 32 * ((jm - g % 4) % 4)
                    piece = tiles[jm][g // 4]
                    if shift:
                        piece = pltpu.roll(piece, shift, 1)
                    total = piece if total is None else jnp.where(block == jm, piece, total)
                target[g, pl.ds(row0 + i * TILES, TILES), t * 128 : (t + 1) * 128] = total.astype(target.dtype)
        return carry

    loop(8, step)


def compute_kernel(
    x_ref, taps_ref, w1_ref, w2t_ref, wr_ref, head_ref, dest_ref, slot_ref, slide_ref, count_ref, targets_ref,
    pred_ref, send_ref, pack_ref,
    taps_pad, g1_ref, g2_ref, gr_ref, low_ref, high_ref, xs_ref, xg_ref, xt_ref, wd_ref, tg_ref, y_ref, f1_ref, w_ref, nb_ref,
    gb_ref, sl_ref, m_ref, pm_ref, w1t_ref, w2_ref, bp_ref, fold_ref,
):
    f2_ref, gn_ref = high_ref, xs_ref
    spread = same_block(256, 32).astype(BF)
    ones = jnp.ones((CHANS, 256), BF)

    def row_sum(values, passes):
        return sum_by(values, ones, passes)[:, 0:CHANS]

    def widen(k, carry):
        rows = pl.ds(k * 512, 512)
        values = x_ref[rows, :].astype(F32)
        low_ref[rows, :] = values[:, 0:128]
        high_ref[rows, 0:64] = values[:, 128:192]
        return carry

    loop(8, widen)

    def regroup(i, carry):
        for j in range(8):
            rows = pl.ds(j * PLANE + i * TILES, TILES)
            xs_ref[rows, 0:128] = low_ref[pl.ds(i * 8 + j, TILES, stride=64), :]
            xs_ref[rows, 128:256] = high_ref[pl.ds(i * 8 + j, TILES, stride=64), :]
        return carry

    loop(8, regroup)

    xg_ref[:, 0 : 3 * TILES, :] = jnp.zeros((GROUPS, 3 * TILES, 256), BF)
    xg_ref[:, 11 * TILES : 14 * TILES, :] = jnp.zeros((GROUPS, 3 * TILES, 256), BF)
    to_groups(xs_ref, xg_ref, 3 * TILES)

    block56 = blocks_of_lanes(56)
    taps_pad[0:49, 0:CHANS] = taps_ref[...]
    taps_low = taps_pad[:, 0:128]
    taps_high = taps_pad[:, 128:256]
    for g in range(GROUPS):
        source = taps_low if g < 4 else taps_high
        total = None
        for jm in range(4):
            shift = 32 * ((jm - g % 4) % 4)
            piece = pltpu.roll(source, shift, 1) if shift else source
            total = piece if total is None else jnp.where(block56 == jm, piece, total)
        for a in range(7):
            tg_ref[g, a, 0:4, :] = jnp.zeros((4, 128), F32)
            tg_ref[g, a, 4:11, :] = total[a * 7 : a * 7 + 7, :]
            tg_ref[g, a, 11:16, :] = jnp.zeros((5, 128), F32)
    same = lax.broadcasted_iota(jnp.int32, (32, 128), 0) == lax.broadcasted_iota(jnp.int32, (32, 128), 1) % 32
    block32 = blocks_of_lanes(32)

    def bands(g):
        for a in range(7):
            for d in range(-4, 8):
                total = None
                for jm in range(4):
                    b = d - jm + 3
                    if b < 0 or b > 6:
                        continue
                    row = jnp.broadcast_to(tg_ref[g, a, 4 + b : 5 + b, :], (32, 128))
                    keep = same & (block32 == jm)
                    total = jnp.where(keep, row, 0.0) if total is None else jnp.where(keep, row, total)
                if total is None:
                    total = jnp.zeros((32, 128), F32)
                pieces = parts_of(total)[:SPLIT]
                for p in range(SPLIT):
                    if d >= 0:
                        wd_ref[a, p, d * 32 : d * 32 + 32, 0:128] = pieces[p]
                    if d + 4 < 8:
                        wd_ref[a, p, (d + 4) * 32 : (d + 4) * 32 + 32, 128:256] = pieces[p]

    def convolve(g, carry):
        bands(g)
        total = None
        for a in range(7):
            lhs = xg_ref[g, a * TILES : a * TILES + PLANE, :]
            for p in range(SPLIT):
                found = dot(lhs, wd_ref[a, p])
                total = found if total is None else total + found
        y_ref[g] = total
        xt_ref[g, 0, :, 128:768] = jnp.transpose(xg_ref[g, 128:768, :], (1, 0))
        xt_ref[g, 1, :, 128:640] = jnp.transpose(xg_ref[g, 192:704, :], (1, 0))
        xt_ref[g, 0, :, 0:128] = jnp.zeros((256, 128), BF)
        xt_ref[g, 0, :, 768:896] = jnp.zeros((256, 128), BF)
        xt_ref[g, 1, :, 0:128] = jnp.zeros((256, 128), BF)
        xt_ref[g, 1, :, 640:896] = jnp.zeros((256, 256), BF)
        return carry

    loop(GROUPS, convolve)

    def first_norm(k, carry):
        rows = pl.ds(k * LR, LR)
        total = y_ref[0, rows, :]
        for g in range(1, GROUPS):
            total = total + y_ref[g, rows, :]
        mean = sum_by(total, spread, 2) * (1.0 / CHANS)
        square = None
        for g in range(GROUPS):
            centered = y_ref[g, rows, :] - mean
            y_ref[g, rows, :] = centered
            square = centered * centered if square is None else square + centered * centered
        factor = lax.rsqrt(sum_by(square, spread, 1) * (1.0 / CHANS) + norm_eps)
        f1_ref[rows, :] = factor
        for g in range(GROUPS):
            y_ref[g, rows, :] = y_ref[g, rows, :] * factor
        return carry

    loop(PLANE // LR, first_norm)

    block64 = blocks_of_lanes(TILES)

    def to_lanes(i, carry):
        rows = pl.ds(i * TILES, TILES)
        for t in range(2):
            tiles = [y_ref[g, rows, t * 128 : (t + 1) * 128] for g in range(GROUPS)]
            for jm in range(4):
                where = pl.ds((4 * t + jm) * PLANE + i * TILES, TILES)
                for half, picks in enumerate(((0, 1, 2, 3), (4, 5))):
                    total = None
                    for g in picks:
                        shift = 32 * ((g % 4 - jm) % 4)
                        piece = pltpu.roll(tiles[g], shift, 1) if shift else tiles[g]
                        total = piece if total is None else jnp.where(block64 == g % 4, piece, total)
                    nb_ref[where, half * 128 : half * 128 + 128] = total.astype(BF)
        return carry

    loop(8, to_lanes)

    pm_ref[...] = jnp.zeros_like(pm_ref)
    w1t_ref[...] = jnp.transpose(w1_ref[...], (1, 0))
    w2_ref[...] = jnp.transpose(w2t_ref[...], (1, 0))

    def block_step(k, carry):
        rows = pl.ds(k * CH, CH)
        low = nb_ref[rows, 0:CHANS]
        branch = None
        for part in range(HIDDEN // HP):
            cols = slice(part * HP, part * HP + HP)
            hidden = dot(low, w1_ref[:, cols])
            active, slope = gelu_pair(hidden)
            active = active.astype(BF)
            gb_ref[rows, cols] = active
            sl_ref[rows, cols] = slope.astype(BF)
            found = dot(active, w2_ref[cols, :])
            branch = found if branch is None else branch + found
        summed = xs_ref[rows, 0:CHANS] + branch
        centered = summed - row_sum(summed, 2) * (1.0 / CHANS)
        factor = lax.rsqrt(row_sum(centered * centered, 1) * (1.0 / CHANS) + norm_eps)
        normed = centered * factor
        m_ref[rows, 0:CHANS] = normed
        f2_ref[rows, :] = factor[:, 0:128]
        rounded = normed.astype(BF).astype(F32)
        lateral = lax.rem(k // (PLANE // CH), 2)
        for u in range(2):
            total = None
            for i in range(u, CH // TILES, 2):
                piece = rounded[i * TILES : (i + 1) * TILES, :]
                total = piece if total is None else total + piece
            pm_ref[u, lateral] += total
        return carry

    loop(8 * PLANE // CH, block_step)

    pooled = [pm_ref[u, v] * (1.0 / 16.0) for u in range(2) for v in range(2)]
    split = [parts_of(piece) for piece in pooled]
    reduced = None
    for q in range(4):
        stacked = jnp.concatenate(split[q], axis=0)
        found = dot(stacked, wr_ref[q * CHANS : (q + 1) * CHANS, :])
        found = found[0:TILES] + found[TILES : 2 * TILES] + found[2 * TILES :]
        reduced = found if reduced is None else reduced + found
    embedded, third = norm_rows(reduced)
    slide_row = slide_ref[...]
    member = (slide_row == lax.broadcasted_iota(jnp.int32, (8, TILES), 0)).astype(F32)
    eye = lax.broadcasted_iota(jnp.int32, (TILES, TILES), 0) == lax.broadcasted_iota(jnp.int32, (TILES, TILES), 1)
    count_rows = jnp.broadcast_to(count_ref[...].astype(F32), (8, 4))
    slide_of = lax.broadcasted_iota(jnp.int32, (8, 4), 0)
    counts = jnp.sum(
        jnp.where(slide_of == lax.broadcasted_iota(jnp.int32, (8, 4), 1), count_rows, 0.0), axis=1, keepdims=True
    )
    counts = jnp.where(slide_of[:, 0:1] < 4, counts, 1.0)
    exact = functools.partial(jnp.dot, precision=lax.Precision.HIGHEST, preferred_element_type=F32)
    pooled_slides = exact(member, embedded) / counts
    predicted = exact(pooled_slides, head_ref[...])
    pred_ref[...] = predicted[0:4]
    missed = predicted[0:4] - targets_ref[...]
    missed = jnp.concatenate([missed, jnp.zeros((4, missed.shape[1]), F32)], axis=0)
    back_pooled = (
        lax.dot_general(
            missed, head_ref[...], (((1,), (1,)), ((), ())), precision=lax.Precision.HIGHEST, preferred_element_type=F32
        )
        / counts
    )
    cotangent = lax.dot_general(
        member, back_pooled, (((0,), (0,)), ((), ())), precision=lax.Precision.HIGHEST, preferred_element_type=F32
    )
    back = third * (cotangent - lane_mean(cotangent) - embedded * lane_mean(cotangent * embedded))
    back_parts = parts_of(back)
    stacked_back = jnp.concatenate(back_parts, axis=0)
    for q in range(4):
        piece = dot_nt(stacked_back, wr_ref[q * CHANS : (q + 1) * CHANS, :])
        piece = (piece[0:TILES] + piece[TILES : 2 * TILES] + piece[2 * TILES :]) * (1.0 / 16.0)
        bp_ref[q // 2, q % 2] = piece - lane_mean(piece)
        rows_q = jnp.concatenate([split[q][0], split[q][1], split[q][0]], axis=0)
        cols_q = jnp.concatenate([back_parts[0], back_parts[0], back_parts[1]], axis=0)
        gr_ref[q * CHANS : (q + 1) * CHANS, :] = dot_tn(rows_q, cols_q)

    dest_row = dest_ref[...]
    dest_col = jnp.sum(jnp.where(eye, jnp.broadcast_to(dest_row, (TILES, TILES)).astype(F32), 0.0), axis=1, keepdims=True)
    first_index = lax.broadcasted_iota(jnp.int32, (TILES, TILES), 0)
    second_index = lax.broadcasted_iota(jnp.int32, (TILES, TILES), 1)
    dest_f = dest_row.astype(F32)
    earlier = (dest_col == dest_f) & (first_index < second_index)
    rank = jnp.sum(earlier.astype(F32), axis=0, keepdims=True)
    slot_f = slot_ref[...].astype(F32) + 1.0
    slot_col = jnp.sum(jnp.where(eye, jnp.broadcast_to(slot_f, (TILES, TILES)), 0.0), axis=1, keepdims=True)
    emb_parts = parts_of(embedded)
    peer = lax.broadcasted_iota(jnp.int32, (32, TILES), 0).astype(F32)
    for r in range(2):
        choose = ((peer == dest_f) & (rank == float(r))).astype(BF)
        picked = dot(choose, emb_parts[0]) + dot(choose, emb_parts[1]) + dot(choose, emb_parts[2])
        for q in range(3):
            send_ref[pl.ds(r * 4 + q, 32, stride=8), :] = picked[:, q * 128 : (q + 1) * 128]
        send_ref[pl.ds(r * 4 + 3, 32, stride=8), :] = dot(choose, jnp.broadcast_to(slot_col, (TILES, 128)).astype(BF))

    g1_ref[...] = jnp.zeros_like(g1_ref)
    g2_ref[...] = jnp.zeros_like(g2_ref)

    def back_step(k, carry):
        rows = pl.ds(k * CH, CH)
        lateral = lax.rem(k // (PLANE // CH), 2)
        patch = [bp_ref[u, lateral] for u in range(2)]
        incoming = jnp.concatenate([patch[i % 2] for i in range(CH // TILES)], axis=0)
        normed = m_ref[rows, 0:CHANS]
        factor = f2_ref[rows, :]
        factor = jnp.concatenate([factor, factor[:, 0 : CHANS - 128]], axis=1)
        back_sum = factor * (incoming - normed * (row_sum(incoming * normed, 1) * (1.0 / CHANS)))
        low = back_sum.astype(BF)
        active = gb_ref[rows, :]
        g2_ref[...] += dot_tn(low, active)
        nb = nb_ref[rows, 0:CHANS]
        normal = None
        for part in range(HIDDEN // HP):
            cols = slice(part * HP, part * HP + HP)
            back_hidden = (dot(low, w2t_ref[:, cols]) * sl_ref[rows, cols].astype(F32)).astype(BF)
            g1_ref[:, cols] += dot_tn(nb, back_hidden)
            found = dot(back_hidden, w1t_ref[cols, :])
            normal = found if normal is None else normal + found
        gn_ref[rows, 0:CHANS] = normal
        return carry

    loop(8 * PLANE // CH, back_step)

    to_groups(gn_ref, w_ref, 0)

    def first_back(k, carry):
        rows = pl.ds(k * LR, LR)
        total = None
        product = None
        for g in range(GROUPS):
            w = w_ref[g, rows, :]
            total = w if total is None else total + w
            scaled = w * y_ref[g, rows, :]
            product = scaled if product is None else product + scaled
        mean = sum_by(total, spread, 2) * (1.0 / CHANS)
        product = sum_by(product, spread, 1) * (1.0 / CHANS)
        factor = f1_ref[rows, :]
        for g in range(GROUPS):
            found = factor * (w_ref[g, rows, :] - mean - y_ref[g, rows, :] * product)
            xg_ref[g, rows, :] = found.astype(BF)
        return carry

    loop(PLANE // LR, first_back)
    block8 = blocks_of_lanes(8)
    same8 = [
        (lax.broadcasted_iota(jnp.int32, (8, 128), 0) + 8 * v) == lax.broadcasted_iota(jnp.int32, (8, 128), 1) % 32
        for v in range(4)
    ]

    def tap_step(g, carry):
        right = xg_ref[g, 0:PLANE, :]
        for a in range(7):
            lane0 = (a * TILES) // 128 * 128
            left = xt_ref[g, a % 2, :, lane0 : lane0 + PLANE]
            found = dot(left, right)
            sums = {}
            for j in range(8):
                for t in range(2):
                    total = None
                    for v in range(4):
                        piece = found[j * 32 + v * 8 : j * 32 + v * 8 + 8, t * 128 : (t + 1) * 128]
                        piece = jnp.where(same8[v], piece, 0.0)
                        total = piece if total is None else total + piece
                    sums[j, t] = total
            for b in range(7):
                total = None
                for t in range(2):
                    inner = jnp.zeros((8, 128), F32)
                    for jm in range(4):
                        j = 4 * t + jm + b - 3
                        if 0 <= j < 8:
                            inner = jnp.where(block8 == jm, sums[j, t], inner)
                    total = inner if total is None else total + inner
                total = total + pltpu.roll(total, 64, 1)
                total = total + pltpu.roll(total, 32, 1)
                fold_ref[g, a * 7 + b : a * 7 + b + 1, :] = jnp.sum(total, axis=0, keepdims=True)
        return carry

    loop(GROUPS, tap_step)
    block49 = blocks_of_lanes(56)
    for half, picks in enumerate(((0, 1, 2, 3), (4, 5))):
        total = jnp.zeros((56, 128), F32)
        for g in picks:
            total = jnp.where(block49 == g % 4, fold_ref[g], total)
        for band in range(7):
            pack_ref[band * 2 + half, 72:80, :] = total[band * 8 : band * 8 + 8, :]
    pack_ref[14:64, 72:80, :] = jnp.zeros((50, 8, 128), F32)
    for k in range(32):
        for l in range(3):
            pack_ref[k, l * 24 : l * 24 + 24, :] = gr_ref[k * 24 : k * 24 + 24, l * 128 : l * 128 + 128]
    for k in range(16):
        for l in range(3):
            lane = (k % 2) * 384 + l * 128
            row = k // 2 * 24
            pack_ref[32 + k, l * 24 : l * 24 + 24, :] = g1_ref[row : row + 24, lane : lane + 128]
            pack_ref[48 + k, l * 24 : l * 24 + 24, :] = g2_ref[row : row + 24, lane : lane + 128]


SPLIT = 2
CH = 512
LR = 256
HP = 256


def compute(x, taps, w1, w2t, wr, head, dest, slot, slide, count, targets):
    shapes = (
        jax.ShapeDtypeStruct((4, 256), F32),
        jax.ShapeDtypeStruct((256, 128), F32),
        jax.ShapeDtypeStruct((64, 80, 128), F32),
    )
    rows = 8 * PLANE
    scratch = [
        pltpu.VMEM((56, 256), F32),
        pltpu.VMEM((CHANS, HIDDEN), F32),
        pltpu.VMEM((CHANS, HIDDEN), F32),
        pltpu.VMEM((4 * CHANS, WIDTH), F32),
        pltpu.VMEM((rows, 128), F32),
        pltpu.VMEM((rows, 128), F32),
        pltpu.VMEM((rows, 256), F32),
        pltpu.VMEM((GROUPS, 14 * TILES, 256), BF),
        pltpu.VMEM((GROUPS, 2, 256, 896), BF),
        pltpu.VMEM((7, SPLIT, 256, 256), BF),
        pltpu.VMEM((GROUPS, 7, 16, 128), F32),
        pltpu.VMEM((GROUPS, PLANE, 256), F32),
        pltpu.VMEM((PLANE, 256), F32),
        pltpu.VMEM((GROUPS, PLANE, 256), F32),
        pltpu.VMEM((rows, 256), BF),
        pltpu.VMEM((rows, HIDDEN), BF),
        pltpu.VMEM((rows, HIDDEN), BF),
        pltpu.VMEM((rows, 256), F32),
        pltpu.VMEM((2, 2, TILES, CHANS), F32),
        pltpu.VMEM((HIDDEN, CHANS), BF),
        pltpu.VMEM((HIDDEN, CHANS), BF),
        pltpu.VMEM((2, 2, TILES, CHANS), F32),
        pltpu.VMEM((GROUPS, 56, 128), F32),
    ]
    return pl.pallas_call(
        compute_kernel,
        out_shape=shapes,
        in_specs=[pl.BlockSpec(memory_space=pltpu.VMEM)] * 11,
        out_specs=tuple(pl.BlockSpec(memory_space=pltpu.VMEM) for _ in shapes),
        scratch_shapes=scratch,
        compiler_params=pltpu.CompilerParams(vmem_limit_bytes=62 * 1024 * 1024),
        name="encode_and_gradients",
    )(x, taps, w1, w2t, wr, head, dest, slot, slide, count, targets)


def sum_kernel(pack_ref, send_ref, all_ref, got_ref, core_out, core_in, own_ref, plane_out, plane_in, z_out, z_in, send_sems, recv_sems):
    bulk = lax.axis_index("bulk")
    slide = lax.axis_index("slide")
    x, y = bulk // 8, bulk % 8
    z, core = slide // 2, slide % 2

    def place(bx, by, bz, bc):
        return (bx * 8 + by, bz * 2 + bc)

    mate = place(x, y, z, 1 - core)
    z_peers = [((z + o) % 8) for o in range(1, 8)]
    b_peers = [((bulk + o) % 32) for o in range(1, 32)]
    barrier = pltpu.get_barrier_semaphore()
    everyone = [mate] + [(b, slide) for b in b_peers] + [place(x, y, p, core) for p in z_peers]
    for device in everyone:
        pl.semaphore_signal(barrier, inc=1, device_id=device, device_id_type=pl.DeviceIdType.MESH)
    counter = [0]

    def copy(source, target, device):
        k = counter[0]
        counter[0] += 1
        made = pltpu.make_async_remote_copy(
            src_ref=source, dst_ref=target, send_sem=send_sems.at[k], recv_sem=recv_sems.at[k],
            device_id=device, device_id_type=pl.DeviceIdType.MESH,
        )
        made.start()
        return made

    def finish(copies):
        for made in copies:
            made.wait_recv()

    def pack(k, carry):
        core_out[k] = pack_ref[(1 - core) * 32 + k].astype(BF)
        return carry

    lax.fori_loop(0, 32, pack, 0, unroll=8)
    pl.semaphore_wait(barrier, len(everyone))
    started = [copy(core_out, core_in, mate)]
    finish(started)

    def add_core(k, carry):
        total = pack_ref[core * 32 + k] + core_in[k].astype(F32)
        own_ref[k] = total
        plane_out[k] = total.astype(BF)
        return carry

    lax.fori_loop(0, 32, add_core, 0, unroll=8)
    step = [copy(plane_out.at[p], plane_in.at[o], (p, slide)) for o, p in enumerate(b_peers)]
    started += step
    tiles = [copy(send_ref.at[p], got_ref.at[bulk], (p, slide)) for p in b_peers]
    got_ref[bulk] = send_ref[bulk]
    finish(step)
    total = own_ref[bulk]
    for o in range(31):
        total = total + plane_in[o].astype(F32)
    z_out[...] = total.astype(ZT)
    step = [copy(z_out, z_in.at[z], place(x, y, p, core)) for p in z_peers]
    started += step
    z_in[z] = z_out[...]
    finish(step)
    total = z_in[0].astype(F32)
    for o in range(1, 8):
        total = total + z_in[o].astype(F32)
    mine = core * 32 + bulk
    all_ref[mine] = total.astype(BF)
    step = [copy(all_ref.at[mine], all_ref.at[mine], (p, slide)) for p in b_peers]
    started += step
    finish(step)
    half = all_ref.at[pl.ds(core * 32, 32)]
    step = [copy(half, half, mate)]
    started += step
    finish(step)
    finish(tiles)
    for made in started + tiles:
        made.wait_send()


ZT = BF


def sum_everywhere(pack, send):
    vmem = pl.BlockSpec(memory_space=pltpu.VMEM)
    return pl.pallas_call(
        sum_kernel,
        out_shape=(jax.ShapeDtypeStruct((64, 80, 128), BF), jax.ShapeDtypeStruct((32, 8, 128), F32)),
        in_specs=[vmem, vmem],
        out_specs=(vmem, vmem),
        scratch_shapes=[
            pltpu.VMEM((32, 80, 128), BF),
            pltpu.VMEM((32, 80, 128), BF),
            pltpu.VMEM((32, 80, 128), F32),
            pltpu.VMEM((32, 80, 128), BF),
            pltpu.VMEM((31, 80, 128), BF),
            pltpu.VMEM((80, 128), ZT),
            pltpu.VMEM((8, 80, 128), ZT),
            pltpu.SemaphoreType.DMA((102,)),
            pltpu.SemaphoreType.DMA((102,)),
        ],
        compiler_params=pltpu.CompilerParams(
            collective_id=0, has_side_effects=True, vmem_limit_bytes=40 * 1024 * 1024
        ),
        name="sum_gradients",
    )(pack, send.reshape(32, 8, 128))


def unpack_kernel(all_ref, got_ref, cache_ref, gt_ref, g1_ref, g2_ref, gr_ref):
    for k in range(32):
        values = all_ref[k, 0:72, :].astype(F32)
        for l in range(3):
            gr_ref[k * 24 : k * 24 + 24, l * 128 : l * 128 + 128] = values[l * 24 : l * 24 + 24]
    for k in range(16):
        first = all_ref[32 + k, 0:72, :].astype(F32)
        second = all_ref[48 + k, 0:72, :].astype(F32)
        for l in range(3):
            lane = (k % 2) * 384 + l * 128
            row = k // 2 * 24
            g1_ref[row : row + 24, lane : lane + 128] = first[l * 24 : l * 24 + 24]
            g2_ref[row : row + 24, lane : lane + 128] = second[l * 24 : l * 24 + 24]
    for band in range(7):
        left = all_ref[band * 2].astype(F32)[72:80]
        right = all_ref[band * 2 + 1].astype(F32)[72:80]
        count = 8 if band < 6 else 1
        gt_ref[band * 8 : band * 8 + count, 0:128] = left[0:count]
        gt_ref[band * 8 : band * 8 + count, 128:192] = right[0:count, 0:64]
    cache = [jnp.zeros((24, 128), F32) for _ in range(3)]
    for r in range(2):
        slots = jnp.transpose(got_ref[pl.ds(r * 4 + 3, 32, stride=8), :], (1, 0))[0:24]
        wanted = (lax.broadcasted_iota(jnp.int32, (24, 32), 0) + 1).astype(F32)
        choose = (slots == wanted).astype(BF)
        for q in range(3):
            for piece in parts_of(got_ref[pl.ds(r * 4 + q, 32, stride=8), :]):
                cache[q] = cache[q] + dot(choose, piece)
    for q in range(3):
        cache_ref[:, q * 128 : (q + 1) * 128] = cache[q]


def unpack(everything, got):
    vmem = pl.BlockSpec(memory_space=pltpu.VMEM)
    return pl.pallas_call(
        unpack_kernel,
        out_shape=(
            jax.ShapeDtypeStruct((24, WIDTH), F32),
            jax.ShapeDtypeStruct((49, CHANS), F32),
            jax.ShapeDtypeStruct((CHANS, HIDDEN), F32),
            jax.ShapeDtypeStruct((CHANS, HIDDEN), F32),
            jax.ShapeDtypeStruct((4 * CHANS, WIDTH), F32),
        ),
        in_specs=[vmem, vmem],
        out_specs=(vmem,) * 5,
        compiler_params=pltpu.CompilerParams(vmem_limit_bytes=40 * 1024 * 1024),
        name="unpack_gradients",
    )(everything, got.reshape(256, 128))


def prepare(tile_images, destination, encoder_slot, tile_slide, slide_tiles, targets, depth_taps, first_proj, second_proj, reduce_proj, head_proj):
    x = tile_images.reshape(TILES * 64, CHANS)
    return (x, depth_taps, first_proj, second_proj.T, reduce_proj, head_proj, destination.reshape(1, TILES),
            encoder_slot.reshape(1, TILES), tile_slide.reshape(1, TILES), slide_tiles.reshape(1, 4), targets.reshape(4, 256))


def local(*arguments):
    predicted, send, pack = compute(*prepare(*arguments))
    everything, got = sum_everywhere(pack, send)
    cache, gt, g1, g2, gr = unpack(everything, got)
    return predicted[None], cache[None], gt, g1, g2.T, gr


def solution(mesh):
    in_specs = (
        P("slide", "bulk", None, None, None),
        P("slide", "bulk"),
        P("slide", "bulk"),
        P("slide", "bulk"),
        P("slide", "bulk"),
        P("slide", "bulk", None),
        P(),
        P(),
        P(),
        P(),
        P(),
    )
    out_specs = (P("slide", "bulk", None), P("slide", "bulk", None), P(), P(), P(), P())
    return jax.shard_map(local, mesh=mesh, in_specs=in_specs, out_specs=out_specs, check_vma=False)
```
